256 devices in a mesh: seq: 128 (over y, z, x_hi, core), head: 2 (over x_lo).
Axes of the slice: x: 4 (x_hi: 2, x_lo: 2; x = x_hi * 2 + x_lo), y: 4, z: 8, core: 2. Of those that a mesh axis runs over, the one named last changes fastest.
Arguments:
- queries: bfloat16 [131072, 1024], P('seq', 'head'), may hold values from -6 to 6
- key_rows: bfloat16 [131072, 1024], P('seq', 'head'), may hold values from -6 to 6
- value_rows: bfloat16 [131072, 1024], P('seq', 'head'), may hold values from -24 to 24
- out_proj: bfloat16 [1024, 1024], P('head'), may hold values from -0.1875 to 0.1875
- grad_out: bfloat16 [131072, 1024], P('seq', 'head'), may hold values from -24 to 24
- band_blocks: int32 [2048], P('seq'), may hold values from 1 to 9, as said below
- column_reach: int32 [2048], P('seq'), may hold values from 2 to 256, as said below
Outputs:
- output: bfloat16 [131072, 1024], P('seq', 'head')
- query_grad: bfloat16 [131072, 1024], P('seq', 'head')
- key_grad: bfloat16 [131072, 1024], P('seq', 'head')
- value_grad: bfloat16 [131072, 1024], P('seq', 'head')
- proj_grad: float32 [1024, 1024], P('head', 'seq')
The draws below stay inside these ranges and needn't reach their ends.
Inputs may be any that keep to these rules, and one draw needn't show every extreme that they name: `band_blocks`: the value 9 occurs in every draw. `column_reach`: the value 256 occurs in every draw.
All inputs are finite; a program needn't handle non-finite values.
Results may differ from the reference program's by a relative error of at most 0.015.
Values may be sent and summed in bfloat16 or wider, within the bound.
A program may use at most 128 MiB of HBM per device.

```python
import math
import jax
import jax.numpy as jnp
from jax import lax

HEAD_DIM = 64
STRIDE = 512
BLOCK = 64
D = 1024
HALF = 4
ROWS = 256
TOKENS = 131072
NBLK = 2048
BAND_MAX = 9
N_HEAD = 2


def draw_queries(key, part):
    key = jax.random.fold_in(key, 3)
    field = jnp.clip(jax.random.normal(key, (TOKENS, D), jnp.float32), -6.0, 6.0)
    return field.astype(jnp.bfloat16)


def draw_key_rows(key, part):
    key = jax.random.fold_in(key, 5)
    field = jnp.clip(jax.random.normal(key, (TOKENS, D), jnp.float32), -6.0, 6.0)
    return field.astype(jnp.bfloat16)


def draw_band_blocks(key, part):
    key = jax.random.fold_in(key, 7)
    value_key, spot_key = jax.random.split(key)
    drawn = jax.random.randint(value_key, (NBLK,), 1, BAND_MAX + 1)
    spot = jax.random.randint(spot_key, (), 0, NBLK)
    return jnp.where(jnp.arange(NBLK) == spot, BAND_MAX, drawn).astype(jnp.int32)


def draw_column_reach(key, part):
    key = jax.random.fold_in(key, 9)
    value_key, spot_key = jax.random.split(key)
    drawn = jax.random.randint(value_key, (NBLK,), 2, ROWS + 1)
    spot = jax.random.randint(spot_key, (), 0, NBLK)
    return jnp.where(jnp.arange(NBLK) == spot, ROWS, drawn).astype(jnp.int32)


def with_spikes(values, key, source, target, blocks, factor):
    owner, partner = [(jnp.arange(values.shape[position]) // (values.shape[position] // blocks)).reshape([-1 if axis == position else 1 for axis in range(values.ndim)]) for position in (source, target)]
    chosen = jax.random.permutation(key, blocks)[partner]
    strong = (owner == chosen) | (owner == (partner + blocks // 2) % blocks)
    return jnp.where(strong, factor * values, values)


def steps_of(stream_key, dims, shards, low, largest):
    factor_of = 1.0
    for position, shards_of in shards:
        draws = jax.random.uniform(jax.random.fold_in(jax.random.fold_in(stream_key, 6), position), (shards_of,), jnp.float32, low / len(shards), largest / len(shards))
        factor_of = factor_of * jnp.repeat(jnp.exp(draws), dims[position] // shards_of).reshape((-1,) + (1,) * (len(dims) - 1 - position))
    return factor_of


def bell_draw(own_key, extent, scale, limit, cuts=(), kind=jnp.bfloat16):
    factor_of = steps_of(own_key, extent, cuts, -0.22, 0.18) if cuts else 1.0
    values = jax.random.normal(own_key, extent, jnp.float32) * scale * factor_of
    return jnp.minimum(jnp.maximum(values, -limit), limit).astype(kind)


def noise_with(rng, extent, width, bound, cuts, heavy, kind=jnp.bfloat16):
    values = width * jax.random.normal(rng, extent, jnp.float32)
    if cuts:
        values = values * steps_of(rng, extent, cuts, -0.22, 0.18)
    return jnp.clip(with_spikes(values, jax.random.fold_in(rng, 3), *heavy), -bound, bound).astype(kind)


def setup_inputs(seed: int = 0) -> dict:
    keys = jax.random.split(jax.random.key(seed), 8)
    queries = draw_queries(jax.random.fold_in(keys[7], 71), 0)
    key_rows = draw_key_rows(jax.random.fold_in(keys[7], 71), 0)
    value_rows = bell_draw(keys[2], (TOKENS, D), 4.0, 24.0, ((0, 128), (1, 2)))
    out_proj = bell_draw(keys[3], (D, D), D ** -0.5, 0.1875, ((0, 2),))
    grad_out = noise_with(keys[4], (TOKENS, D), 1.0, 24.0, ((0, 128), (1, 2)), (0, 1, 128, 5.5))
    band_blocks = draw_band_blocks(jax.random.fold_in(keys[7], 71), 0)
    column_reach = draw_column_reach(jax.random.fold_in(keys[7], 71), 0)
    return {"queries": queries, "key_rows": key_rows, "value_rows": value_rows, "out_proj": out_proj, "grad_out": grad_out, "band_blocks": band_blocks, "column_reach": column_reach}


MASKED = -1e+30
column_group = 8

def masked_scores(query_part, key_part, allowed):
    raw_scores = jnp.einsum('nbhd,mbhd->bhnm', query_part.astype(jnp.float32), key_part.astype(jnp.float32))
    raw_scores = raw_scores * HEAD_DIM ** (-0.5)
    return jnp.where(allowed[:, None], raw_scores, MASKED)

def attend(query_part, key_part, value_part, allowed):
    scores = masked_scores(query_part, key_part, allowed)
    highest = lax.optimization_barrier(jnp.max(scores, axis=-1, keepdims=True))
    totals = lax.optimization_barrier(jnp.sum(jnp.exp(scores - highest), axis=-1, keepdims=True))
    log_total = highest + jnp.log(totals)
    weights = jnp.exp(scores - log_total).astype(jnp.bfloat16)
    result = jnp.einsum('bhnm,mbhd->nbhd', weights.astype(jnp.float32), value_part.astype(jnp.float32))
    return (result.astype(jnp.bfloat16), log_total[..., 0])

def attend_back(query_part, key_part, value_part, allowed, log_total, d_result, result):
    factor = HEAD_DIM ** (-0.5)
    scores = masked_scores(query_part, key_part, allowed)
    weights_full = jnp.exp(scores - log_total[..., None])
    row_inner = jnp.einsum('nbhd,nbhd->bhn', d_result.astype(jnp.float32), result.astype(jnp.float32))
    d_weights = jnp.einsum('nbhd,mbhd->bhnm', d_result.astype(jnp.float32), value_part.astype(jnp.float32))
    d_scores = (weights_full * (d_weights - row_inner[..., None])).astype(jnp.bfloat16).astype(jnp.float32)
    d_query = jnp.einsum('bhnm,mbhd->nbhd', d_scores, key_part.astype(jnp.float32)) * factor
    d_key = jnp.einsum('bhnm,nbhd->mbhd', d_scores, query_part.astype(jnp.float32)) * factor
    weights_low = weights_full.astype(jnp.bfloat16).astype(jnp.float32)
    d_value = jnp.einsum('bhnm,nbhd->mbhd', weights_low, d_result.astype(jnp.float32))
    return (d_query, d_key, d_value)

def heads_apart(matrix):
    length_rows = matrix.shape[0]
    grouped = matrix.reshape(length_rows, N_HEAD, 2, HALF, HEAD_DIM)
    return (grouped[:, :, 0].reshape(length_rows, N_HEAD * HALF, HEAD_DIM), grouped[:, :, 1].reshape(length_rows, N_HEAD * HALF, HEAD_DIM))

def heads_joined(band_part, column_part):
    length_rows = band_part.shape[0]
    stacked = jnp.stack([band_part.reshape(length_rows, N_HEAD, HALF, HEAD_DIM), column_part.reshape(length_rows, N_HEAD, HALF, HEAD_DIM)], axis=2)
    return stacked.reshape(length_rows, D)

def banded_pass(query_all, key_all, value_all, d_all, band_blocks):
    width_heads = query_all.shape[1]
    padding = jnp.zeros((STRIDE, width_heads, HEAD_DIM), key_all.dtype)
    key_pad = jnp.concatenate([padding, key_all], axis=0)
    value_pad = jnp.concatenate([padding, value_all], axis=0)
    band_reach = jnp.repeat(band_blocks, BLOCK)

    def window_step(carry, window):
        begin_at = (window * STRIDE).astype(jnp.int32)
        pos_query = begin_at + jnp.arange(STRIDE, dtype=jnp.int32)
        pos_key = begin_at - STRIDE + jnp.arange(2 * STRIDE, dtype=jnp.int32)
        reach_rows = lax.dynamic_slice_in_dim(band_reach, begin_at, STRIDE)
        blocks_apart = pos_query[:, None] // BLOCK - pos_key[None, :] // BLOCK
        allowed = ((pos_key[None, :] <= pos_query[:, None]) & (pos_key[None, :] >= 0) & (blocks_apart < reach_rows[:, None]))[None]
        query_part = lax.dynamic_slice_in_dim(query_all, begin_at, STRIDE)[:, None]
        key_part = lax.dynamic_slice_in_dim(key_pad, begin_at, 2 * STRIDE)[:, None]
        value_part = lax.dynamic_slice_in_dim(value_pad, begin_at, 2 * STRIDE)[:, None]
        d_part = lax.dynamic_slice_in_dim(d_all, begin_at, STRIDE)[:, None]
        result, log_total = attend(query_part, key_part, value_part, allowed)
        d_query, d_key, d_value = attend_back(query_part, key_part, value_part, allowed, log_total, d_part, result)
        key_grad = d_key[STRIDE:, 0] + carry[0]
        value_grad = d_value[STRIDE:, 0] + carry[1]
        return ((d_key[:STRIDE, 0], d_value[:STRIDE, 0]), (result[:, 0], d_query[:, 0].astype(jnp.bfloat16), key_grad.astype(jnp.bfloat16), value_grad.astype(jnp.bfloat16)))
    empty = jnp.zeros((STRIDE, width_heads, HEAD_DIM), jnp.float32)
    _, outputs = lax.scan(window_step, (empty, empty), jnp.arange(ROWS, dtype=jnp.int32), reverse=True)
    return tuple((piece.reshape(TOKENS, width_heads, HEAD_DIM) for piece in outputs))

def strided_pass(query_all, key_all, value_all, d_all, column_reach):
    width_heads = query_all.shape[1]
    grids = [matrix.reshape(ROWS, STRIDE, width_heads, HEAD_DIM) for matrix in (query_all, key_all, value_all, d_all)]
    reach_cols = jnp.repeat(column_reach.reshape(ROWS, STRIDE // BLOCK), BLOCK, axis=1)
    row_ids = jnp.arange(ROWS, dtype=jnp.int32)
    rows_apart = row_ids[:, None] - row_ids[None, :]

    def group_step(group):
        begin_at = (group * column_group).astype(jnp.int32)
        parts = [lax.dynamic_slice_in_dim(grid, begin_at, column_group, 1) for grid in grids]
        reach_part = lax.dynamic_slice_in_dim(reach_cols, begin_at, column_group, 1)
        allowed = (rows_apart[None] >= 0) & (rows_apart[None] < jnp.transpose(reach_part)[:, :, None])
        result, log_total = attend(parts[0], parts[1], parts[2], allowed)
        d_query, d_key, d_value = attend_back(parts[0], parts[1], parts[2], allowed, log_total, parts[3], result)
        return (result, d_query.astype(jnp.bfloat16), d_key.astype(jnp.bfloat16), d_value.astype(jnp.bfloat16))
    outputs = lax.map(group_step, jnp.arange(STRIDE // column_group, dtype=jnp.int32))
    return tuple((jnp.moveaxis(piece, 0, 1).reshape(TOKENS, width_heads, HEAD_DIM) for piece in outputs))

def reference(queries, key_rows, value_rows, out_proj, grad_out, band_blocks, column_reach):
    d_attended = jnp.dot(grad_out, out_proj.T, preferred_element_type=jnp.float32).astype(jnp.bfloat16)
    query_band, query_column = heads_apart(queries)
    key_band, key_column = heads_apart(key_rows)
    value_band, value_column = heads_apart(value_rows)
    d_band, d_column = heads_apart(d_attended)
    band_out = banded_pass(query_band, key_band, value_band, d_band, band_blocks)
    column_out = strided_pass(query_column, key_column, value_column, d_column, column_reach)
    attended = heads_joined(band_out[0], column_out[0])
    output = jnp.dot(attended, out_proj, preferred_element_type=jnp.float32).astype(jnp.bfloat16)
    proj_grad = jnp.dot(attended.T, grad_out, preferred_element_type=jnp.float32) * (1.0 / math.sqrt(TOKENS))
    return (output, heads_joined(band_out[1], column_out[1]), heads_joined(band_out[2], column_out[2]), heads_joined(band_out[3], column_out[3]), proj_grad)
```

```python
import functools
import math

import jax
import jax.numpy as jnp
from jax import lax
from jax.experimental import pallas as pl
from jax.experimental.pallas import tpu as pltpu
from jax.sharding import PartitionSpec as P

HEAD_DIM = 64
STRIDE = 512
BLOCK = 64
TILE = 256
MASKED = -1e30
F32 = jnp.float32
BF16 = jnp.bfloat16


def dot(a, b):
    return jnp.dot(a, b, preferred_element_type=F32)


def pair_tile(q, k, v, d, allowed):
    nq = q.shape[0]
    qs = (q.astype(F32) * HEAD_DIM**-0.5).astype(BF16)
    q_t, d_t, k_t, v_t = (m.astype(F32).T.astype(BF16) for m in (qs, d, k, v))
    low = lax.broadcasted_iota(jnp.int32, (nq, 2 * HEAD_DIM), 1) < HEAD_DIM
    blank = jnp.zeros((HEAD_DIM, nq), BF16)
    nothing = jnp.zeros_like(q)
    outs, dqs, dk, dv = [], [], None, None
    for h in range(2):
        mine = slice(h * HEAD_DIM, (h + 1) * HEAD_DIM)

        def alone(m_t):
            return jnp.concatenate([m_t[mine], blank] if h == 0 else [blank, m_t[mine]], axis=0)

        scores = jnp.where(allowed, dot(k, alone(q_t)), MASKED)
        highest = jnp.max(scores, axis=0, keepdims=True)
        weights = jnp.exp(scores - highest)
        weights = weights * (1.0 / jnp.sum(weights, axis=0, keepdims=True))
        low_weights = weights.astype(BF16)
        out_t = dot(v_t[mine], low_weights).astype(BF16).astype(F32)
        delta = jnp.sum(out_t * d_t[mine].astype(F32), axis=0, keepdims=True)
        d_scores = (weights * (dot(v, alone(d_t)) - delta)).astype(BF16)
        outs.append(out_t)
        dqs.append(dot(k_t[mine], d_scores) * HEAD_DIM**-0.5)
        keep = low if h == 0 else jnp.logical_not(low)
        dk_h = dot(d_scores, jnp.where(keep, qs, nothing))
        dv_h = dot(low_weights, jnp.where(keep, d, nothing))
        dk = dk_h if dk is None else dk + dk_h
        dv = dv_h if dv is None else dv + dv_h
    return jnp.concatenate(outs, axis=0).T, jnp.concatenate(dqs, axis=0).T, dk, dv


def band_kernel(q_ref, k_ref, v_ref, d_ref, low_ref, out_ref, dq_ref, dk_ref, dv_ref, dk_sum, dv_sum):
    tokens, width = q_ref.shape
    span = TILE + STRIDE
    for pair in range(width // 128):
        lanes = slice(pair * 128, pair * 128 + 128)
        dk_sum[...] = jnp.zeros_like(dk_sum)
        dv_sum[...] = jnp.zeros_like(dv_sum)

        @pl.loop(0, tokens // TILE)
        def _(step):
            begin = pl.multiple_of(step * TILE, TILE)
            mine, reach = pl.ds(begin, TILE), pl.ds(begin, span)
            key_at = begin + lax.broadcasted_iota(jnp.int32, (span, TILE), 0)
            query_at = STRIDE + begin + lax.broadcasted_iota(jnp.int32, (span, TILE), 1)
            allowed = (key_at <= query_at) & (key_at >= low_ref[:, mine])
            out, dq, dk, dv = pair_tile(
                q_ref[mine, lanes], k_ref[reach, lanes], v_ref[reach, lanes], d_ref[mine, lanes], allowed
            )
            out_ref[mine, lanes] = out.astype(BF16)
            dq_ref[mine, lanes] = dq.astype(BF16)
            dk_sum[reach, :] += dk
            dv_sum[reach, :] += dv

        dk_ref[:, lanes] = dk_sum[...]
        dv_ref[:, lanes] = dv_sum[...]


def column_kernel(qkv_ref, d_ref, reach_ref, res_ref, wide, back):
    devices = qkv_ref.shape[0]
    rows = 2 * devices
    flat = devices * 16
    for t in range(3):
        wide[t] = qkv_ref[:, pl.ds(16 * t, 16), :].astype(F32).reshape(flat, 128)
    wide[3] = d_ref[...].astype(F32).reshape(flat, 128)
    key_at = lax.broadcasted_iota(jnp.int32, (rows, rows), 0)
    query_at = lax.broadcasted_iota(jnp.int32, (rows, rows), 1)

    @pl.loop(0, 8)
    def _(column):
        at = pl.ds(column, rows, stride=8)
        allowed = (key_at <= query_at) & (query_at - key_at < reach_ref[...])
        q, k, v, d = (wide[t, at, :].astype(BF16) for t in range(4))
        for t, value in enumerate(pair_tile(q, k, v, d, allowed)):
            back[t, at, :] = value

    for t in range(4):
        res_ref[:, pl.ds(16 * t, 16), :] = back[t].reshape(devices, 16, 128).astype(BF16)


def vmem(n):
    return [pl.BlockSpec(memory_space=pltpu.VMEM)] * n


def swap_head(x):
    return lax.ppermute(x, "head", [(0, 1), (1, 0)])


def to_messages(matrix, half):
    rows = matrix.shape[0] // STRIDE
    grid = matrix[:, half:].reshape(rows, STRIDE // 8, 8, half // 128, 128)
    return grid.transpose(1, 3, 0, 2, 4).reshape(STRIDE // 8 * (half // 128), rows * 8, 128)


def from_messages(messages, half):
    rows = messages.shape[1] // 8
    grid = messages.reshape(STRIDE // 8, half // 128, rows, 8, 128)
    return grid.transpose(2, 0, 3, 1, 4).reshape(rows * STRIDE, half)


def local(queries, key_rows, value_rows, out_proj, grad_out, band_blocks, column_reach):
    tokens, width = queries.shape
    half = width // 2
    seq_devices = lax.axis_size("seq")
    me = lax.axis_index("seq")
    head = lax.axis_index("head")

    reach = column_reach.reshape(2, STRIDE // BLOCK).T.astype(BF16)
    reach = jnp.repeat(reach, seq_devices // (STRIDE // BLOCK), axis=0)
    reach = jnp.pad(reach[:, None, :], ((0, 0), (0, 7), (0, 126)))
    qkv = jnp.concatenate([to_messages(m, half) for m in (queries, key_rows, value_rows)] + [reach], axis=1)
    qkv = lax.all_to_all(qkv, "seq", 0, 0, tiled=True)
    reach_rows = qkv[:, 48, :2].reshape(1, 2 * seq_devices).astype(jnp.int32)

    grad_other = swap_head(grad_out)
    first = jnp.where(head == 0, grad_out, grad_other)
    second = jnp.where(head == 0, grad_other, grad_out)
    grad_all = jnp.concatenate([first, second], axis=1)
    other_half = lax.dynamic_slice_in_dim(out_proj, (1 - head) * width, width, 1)
    proj_other = swap_head(other_half)
    proj_mine = lax.dynamic_slice_in_dim(out_proj, head * width, width, 1)
    d_attended = lax.dot_general(
        grad_all, out_proj, (((1,), (1,)), ((), ())), preferred_element_type=F32
    ).astype(BF16)
    d_column = lax.all_to_all(to_messages(d_attended, half), "seq", 0, 0, tiled=True)

    rim = jnp.stack([m[tokens - STRIDE :, :half] for m in (key_rows, value_rows)])
    rim = lax.ppermute(rim, "seq", [(i, i + 1) for i in range(seq_devices - 1)])
    key_ext = jnp.concatenate([rim[0], key_rows[:, :half]], axis=0)
    value_ext = jnp.concatenate([rim[1], value_rows[:, :half]], axis=0)
    block_at = jnp.arange(tokens // BLOCK, dtype=jnp.int32)
    lowest = (block_at + STRIDE // BLOCK - band_blocks + 1) * BLOCK
    lowest = jnp.maximum(lowest, jnp.where(me == 0, STRIDE, 0))
    lowest = jnp.repeat(lowest, BLOCK)[None, :]
    flops = 6 * 2 * tokens * (TILE + STRIDE) * half
    band_out, band_dq, band_dk, band_dv = pl.pallas_call(
        band_kernel,
        out_shape=(
            jax.ShapeDtypeStruct((tokens, half), BF16),
            jax.ShapeDtypeStruct((tokens, half), BF16),
            jax.ShapeDtypeStruct((tokens + STRIDE, half), F32),
            jax.ShapeDtypeStruct((tokens + STRIDE, half), F32),
        ),
        in_specs=vmem(5),
        out_specs=tuple(vmem(4)),
        scratch_shapes=[pltpu.VMEM((tokens + STRIDE, 128), F32)] * 2,
        compiler_params=pltpu.CompilerParams(vmem_limit_bytes=40 * 2**20),
        cost_estimate=pl.CostEstimate(flops=4 * flops, bytes_accessed=8 * 2**20, transcendentals=0),
    )(queries[:, :half], key_ext, value_ext, d_attended[:, :half], lowest)
    rim_back = jnp.stack([band_dk[:STRIDE], band_dv[:STRIDE]]).astype(BF16)
    rim_back = lax.ppermute(rim_back, "seq", [(i + 1, i) for i in range(seq_devices - 1)]).astype(F32)

    column_results = pl.pallas_call(
        column_kernel,
        out_shape=jax.ShapeDtypeStruct((seq_devices, 64, 128), BF16),
        in_specs=vmem(3),
        out_specs=vmem(1)[0],
        scratch_shapes=[pltpu.VMEM((4, seq_devices * 16, 128), F32)] * 2,
        compiler_params=pltpu.CompilerParams(vmem_limit_bytes=48 * 2**20),
        cost_estimate=pl.CostEstimate(flops=flops, bytes_accessed=8 * 2**20, transcendentals=0),
    )(qkv, d_column, reach_rows)
    out_back = lax.all_to_all(column_results[:, :16], "seq", 0, 0, tiled=True)
    grads_back = lax.all_to_all(column_results[:, 16:], "seq", 0, 0, tiled=True)

    attended = jnp.concatenate([band_out, from_messages(out_back, half)], axis=1)
    attended_other = swap_head(attended)
    output = (dot(attended, proj_mine) + dot(attended_other, proj_other)).astype(BF16)

    term = lax.dot_general(grad_all, attended, (((0,), (0,)), ((), ())), preferred_element_type=F32)
    parts = term.reshape(4, 8, 2, 2, 8 * width)
    core = lax.rem(me, 2)
    x_hi = lax.rem(me // 2, 2)

    def halve(parts, bit, distance):
        keep = jnp.where(bit == 0, parts[:, :, 0], parts[:, :, 1])
        send = jnp.where(bit == 0, parts[:, :, 1], parts[:, :, 0])
        return keep + lax.ppermute(send, "seq", [(i, i ^ distance) for i in range(seq_devices)])

    parts = halve(parts.transpose(0, 1, 3, 2, 4), core, 1)
    parts = halve(parts, x_hi, 2)
    y_groups = [[y * 32 + rest for y in range(4)] for rest in range(32)]
    z_groups = [[y * 32 + z * 4 + rest for z in range(8)] for y in range(4) for rest in range(4)]
    parts = lax.all_to_all(parts, "seq", 0, 0, axis_index_groups=y_groups, tiled=True).sum(0)
    parts = lax.all_to_all(parts, "seq", 0, 0, axis_index_groups=z_groups, tiled=True).sum(0)
    proj_grad = parts.reshape(8, width).T * (1.0 / math.sqrt(tokens * seq_devices))

    grads = from_messages(grads_back[:, :16], half), from_messages(grads_back[:, 16:32], half), from_messages(grads_back[:, 32:], half)
    query_grad = jnp.concatenate([band_dq, grads[0]], axis=1)

    def joined(ext, rim, column):
        last = (ext[tokens:] + rim).astype(BF16)
        band = jnp.concatenate([ext[STRIDE:tokens].astype(BF16), last], axis=0)
        return jnp.concatenate([band, column], axis=1)

    return (
        output,
        query_grad,
        joined(band_dk, rim_back[0], grads[1]),
        joined(band_dv, rim_back[1], grads[2]),
        proj_grad,
    )


def solution(mesh):
    tokens = P("seq", "head")
    return jax.shard_map(
        local,
        mesh=mesh,
        in_specs=(tokens, tokens, tokens, P("head", None), tokens, P("seq"), P("seq")),
        out_specs=(tokens, tokens, tokens, tokens, P("head", "seq")),
        check_vma=False,
    )
```

```python
import math

import jax
import jax.numpy as jnp
from jax import lax
from jax.experimental import pallas as pl
from jax.experimental.pallas import tpu as pltpu
from jax.sharding import PartitionSpec as P

HEAD_DIM = 64
STRIDE = 512
BLOCK = 64
TILE = 256
MASKED = -1e30
F32 = jnp.float32
BF16 = jnp.bfloat16
MESH = pl.DeviceIdType.MESH
Y, Z, XH, CORES = 4, 8, 2, 2
SEQ = Y * Z * XH * CORES


def dot(a, b):
    return jnp.dot(a, b, preferred_element_type=F32)


def pair_tile(q, k, v, d, allowed):
    nq = q.shape[0]
    qs = (q.astype(F32) * HEAD_DIM**-0.5).astype(BF16)
    q_t, d_t, k_t, v_t = (m.astype(F32).T.astype(BF16) for m in (qs, d, k, v))
    low = lax.broadcasted_iota(jnp.int32, (nq, 2 * HEAD_DIM), 1) < HEAD_DIM
    blank = jnp.zeros((HEAD_DIM, nq), BF16)
    nothing = jnp.zeros_like(q)
    outs, dqs, dk, dv = [], [], None, None
    for h in range(2):
        mine = slice(h * HEAD_DIM, (h + 1) * HEAD_DIM)

        def alone(m_t):
            return jnp.concatenate([m_t[mine], blank] if h == 0 else [blank, m_t[mine]], axis=0)

        scores = jnp.where(allowed, dot(k, alone(q_t)), MASKED)
        highest = jnp.max(scores, axis=0, keepdims=True)
        weights = jnp.exp(scores - highest)
        weights = weights * (1.0 / jnp.sum(weights, axis=0, keepdims=True))
        low_weights = weights.astype(BF16)
        out_t = dot(v_t[mine], low_weights).astype(BF16).astype(F32)
        delta = jnp.sum(out_t * d_t[mine].astype(F32), axis=0, keepdims=True)
        d_scores = (weights * (dot(v, alone(d_t)) - delta)).astype(BF16)
        outs.append(out_t)
        dqs.append(dot(k_t[mine], d_scores) * HEAD_DIM**-0.5)
        keep = low if h == 0 else jnp.logical_not(low)
        dk_h = dot(d_scores, jnp.where(keep, qs, nothing))
        dv_h = dot(low_weights, jnp.where(keep, d, nothing))
        dk = dk_h if dk is None else dk + dk_h
        dv = dv_h if dv is None else dv + dv_h
    return jnp.concatenate(outs, axis=0).T, jnp.concatenate(dqs, axis=0).T, dk, dv


def dot_nt(a, b):
    return lax.dot_general(a, b, (((1,), (1,)), ((), ())), preferred_element_type=F32)


def row_of(count, part, values):
    run = lax.broadcasted_iota(jnp.int32, (1, count), 1) // part
    row = jnp.zeros((1, count), jnp.int32)
    for i, value in enumerate(values):
        row = jnp.where(run == i, value, row)
    return row


def to_messages(x):
    grid = x.astype(F32).reshape(2, STRIDE // 8, 8, 128)
    return jnp.concatenate([grid[0], grid[1]], axis=1).astype(BF16)


def from_messages(m):
    grid = m.astype(F32)
    halves = [grid[:, 8 * r : 8 * r + 8].reshape(STRIDE, 128) for r in range(2)]
    return jnp.concatenate(halves, axis=0).astype(BF16)


def layer_kernel(
    q_ref, k_ref, v_ref, w_ref, g_ref, band_ref, reach_ref,
    out_ref, dq_ref, dk_ref, dv_ref, proj_ref,
    qkv_send, qkv_recv, col_d_send, col_d_recv, reach_all,
    g_other, w_other, rim, rim_send, rim_recv,
    d_att, g_t, dk_sum, dv_sum, wide, back,
    res_out, res_grad, got_out, got_grad, att, att_other,
    term, core_in, core_sum, x_in, x_sum, y_in, y_sum, z_in,
    send, recv,
):
    tokens, width = q_ref.shape
    half = width // 2
    me, head = lax.axis_index("seq"), lax.axis_index("head")
    core, x_hi, z, y = lax.rem(me, 2), lax.rem(me // 2, 2), lax.rem(me // 4, Z), me // (4 * Z)
    seq_at = lambda y, z, x_hi, core: ((y * Z + z) * XH + x_hi) * CORES + core

    def remote(src, dst, n, seq, other=None):
        return pltpu.make_async_remote_copy(
            src_ref=src, dst_ref=dst, send_sem=send.at[n], recv_sem=recv.at[n],
            device_id=(seq, head if other is None else other), device_id_type=MESH,
        )

    barrier = pltpu.get_barrier_semaphore()

    @pl.loop(1, SEQ)
    def _(i):
        pl.semaphore_signal(barrier, inc=1, device_id=(lax.rem(me + i, SEQ), head), device_id_type=MESH)

    pl.semaphore_signal(barrier, inc=1, device_id=(me, 1 - head), device_id_type=MESH)

    lane = lax.broadcasted_iota(jnp.int32, (1, 128), 1)
    mine_reach = row_of(128, 1, [reach_ref[i] for i in range(16)])
    mine_reach = mine_reach.astype(F32)
    reach_all[me] = mine_reach
    for t, ref in enumerate((q_ref, k_ref, v_ref)):
        for hp in range(2):
            lanes = slice(half + hp * 128, half + hp * 128 + 128)
            qkv_send[hp * 64 : hp * 64 + 64, 16 * t : 16 * t + 16, :] = to_messages(ref[:, lanes])
    pl.semaphore_wait(barrier, SEQ)

    swap_g = remote(g_ref, g_other, 0, me, 1 - head)
    swap_g.start()
    their_w = w_ref.at[:, pl.ds(pl.multiple_of((1 - head) * width, 128), width)]
    swap_w = remote(their_w, w_other, 1, me, 1 - head)

    @pl.loop(1, SEQ)
    def _(i):
        to = lax.rem(me + i, SEQ)
        remote(qkv_send.at[to], qkv_recv.at[me], 2, to).start()
        remote(reach_all.at[me], reach_all.at[me], 3, to).start()

    qkv_recv[me] = qkv_send[me]

    for t, ref in enumerate((k_ref, v_ref)):
        rim[t, STRIDE:, :] = ref[:, :half]
    rim_to = remote(rim.at[:, pl.ds(tokens, STRIDE)], rim.at[:, pl.ds(0, STRIDE)], 4, jnp.minimum(me + 1, SEQ - 1))

    @pl.when(me < SEQ - 1)
    def _():
        rim_to.start()

    @pl.when(me == 0)
    def _():
        rim[:, :STRIDE, :] = jnp.zeros((2, STRIDE, half), BF16)

    mine_c = pl.ds(pl.multiple_of(head * width, 128), width)
    other_c = pl.ds(pl.multiple_of((1 - head) * width, 128), width)

    def turn(ref, rows):
        for i in range(tokens // TILE):
            part = slice(i * TILE, i * TILE + TILE)
            g_t[rows, part] = ref[part, :].astype(F32).T.astype(BF16)

    turn(g_ref, mine_c)
    swap_g.wait()

    @pl.loop(0, tokens // TILE)
    def _(i):
        part = pl.ds(pl.multiple_of(i * TILE, TILE), TILE)
        d = dot_nt(g_ref[part, :], w_ref[:, mine_c]) + dot_nt(g_other[part, :], w_ref[:, other_c])
        d_att[part, :] = d.astype(BF16)

    for hp in range(2):
        lanes = slice(half + hp * 128, half + hp * 128 + 128)
        col_d_send[hp * 64 : hp * 64 + 64] = to_messages(d_att[:, lanes])

    @pl.loop(1, SEQ)
    def _(i):
        to = lax.rem(me + i, SEQ)
        remote(col_d_send.at[to], col_d_recv.at[me], 5, to).start()

    col_d_recv[me] = col_d_send[me]
    swap_w.start()
    turn(g_other, other_c)

    @pl.when(me < SEQ - 1)
    def _():
        rim_to.wait_send()

    @pl.when(me > 0)
    def _():
        rim_to.wait_recv()

    blocks = tokens // BLOCK
    span = TILE + STRIDE
    edge = jnp.where(me == 0, STRIDE, 0)
    for pair in range(2):
        lanes = slice(pair * 128, pair * 128 + 128)
        dk_sum[pair] = jnp.zeros((tokens + STRIDE, 128), F32)
        dv_sum[pair] = jnp.zeros((tokens + STRIDE, 128), F32)

    @pl.loop(0, tokens // TILE)
    def _(step):
        begin = pl.multiple_of(step * TILE, TILE)
        mine, span_at = pl.ds(begin, TILE), pl.ds(begin, span)
        key_at = lax.broadcasted_iota(jnp.int32, (span, TILE), 0)
        query_at = STRIDE + lax.broadcasted_iota(jnp.int32, (span, TILE), 1)
        block_at = query_at[:1] // BLOCK
        count = row_of(TILE, BLOCK, [band_ref[step * (TILE // BLOCK) + i] for i in range(TILE // BLOCK)])
        lowest = jnp.maximum((block_at - count + 1) * BLOCK, edge - begin)
        allowed = (key_at <= query_at) & (key_at >= lowest)
        for pair in range(2):
            lanes = slice(pair * 128, pair * 128 + 128)
            out, dq, dk, dv = pair_tile(
                q_ref[mine, lanes], rim[0, span_at, lanes], rim[1, span_at, lanes], d_att[mine, lanes], allowed
            )
            att[mine, lanes] = out.astype(BF16)
            dq_ref[mine, lanes] = dq.astype(BF16)
            dk_sum[pair, span_at, :] += dk
            dv_sum[pair, span_at, :] += dv

    for pair in range(2):
        lanes = slice(pair * 128, pair * 128 + 128)
        rim_send[0, :, lanes] = dk_sum[pair, :STRIDE, :].astype(BF16)
        rim_send[1, :, lanes] = dv_sum[pair, :STRIDE, :].astype(BF16)
    rim_back = remote(rim_send, rim_recv, 6, jnp.maximum(me - 1, 0))

    @pl.when(me > 0)
    def _():
        rim_back.start()

    @pl.when(me == SEQ - 1)
    def _():
        rim_recv[...] = jnp.zeros((2, STRIDE, half), BF16)

    def wait_all(src, dst, n):
        everyone = remote(src.at[pl.ds(0, SEQ - 1)], dst.at[pl.ds(0, SEQ - 1)], n, lax.rem(me + 1, SEQ))
        everyone.wait_send()
        everyone.wait_recv()

    wait_all(reach_all, reach_all, 3)
    wait_all(qkv_send, qkv_recv, 2)
    wait_all(col_d_send, col_d_recv, 5)
    for t in range(3):
        wide[t] = qkv_recv[:, 16 * t : 16 * t + 16, :].astype(F32).reshape(16 * SEQ, 128)
    wide[3] = col_d_recv[...].astype(F32).reshape(16 * SEQ, 128)
    table = reach_all[...].reshape(SEQ, 128).T
    block = lax.rem(me, 64) // 8
    row_at = lax.broadcasted_iota(jnp.int32, (128, SEQ), 0)
    reach = jnp.concatenate(
        [jnp.sum(jnp.where(row_at == block + 8 * r, table, 0.0), axis=0, keepdims=True) for r in range(2)], axis=1
    ).astype(jnp.int32)
    rows = 2 * SEQ

    def image_row(axis):
        i = lax.broadcasted_iota(jnp.int32, (rows, rows), axis)
        return 2 * lax.rem(i, SEQ) + i // SEQ

    @pl.loop(0, 8)
    def _(column):
        apart = image_row(1) - image_row(0)
        allowed = (apart >= 0) & (apart < reach)
        at = [pl.ds(column + 8 * r, SEQ, stride=16) for r in range(2)]
        q, k, v, d = (
            jnp.concatenate([wide[t, at[0], :], wide[t, at[1], :]], axis=0).astype(BF16) for t in range(4)
        )
        for t, value in enumerate(pair_tile(q, k, v, d, allowed)):
            for r in range(2):
                back[t, at[r], :] = value[r * SEQ : r * SEQ + SEQ]

    res_out[...] = back[0].reshape(SEQ, 16, 128).astype(BF16)

    @pl.loop(1, SEQ)
    def _(i):
        to = lax.rem(me + i, SEQ)
        remote(res_out.at[to], got_out.at[me], 7, to).start()

    got_out[me] = res_out[me]
    for t in range(3):
        res_grad[:, 16 * t : 16 * t + 16, :] = back[t + 1].reshape(SEQ, 16, 128).astype(BF16)

    @pl.loop(1, SEQ)
    def _(i):
        to = lax.rem(me + i, SEQ)
        remote(res_grad.at[to], got_grad.at[me], 8, to).start()

    got_grad[me] = res_grad[me]

    wait_all(res_out, got_out, 7)
    for hp in range(2):
        att[:, half + hp * 128 : half + hp * 128 + 128] = from_messages(got_out[hp * 64 : hp * 64 + 64])
    swap_att = remote(att, att_other, 9, me, 1 - head)
    swap_att.start()

    @pl.loop(0, 2 * width // TILE)
    def _(i):
        part = pl.ds(pl.multiple_of(i * TILE, TILE), TILE)
        term[pl.ds(8 * i, 8)] = dot(g_t[part, :], att[...]).reshape(8, XH, CORES, 8, width)

    copy = remote(term.at[:, :, 1 - core], core_in, 10, me + 1 - 2 * core)
    copy.start()
    copy.wait()

    @pl.loop(0, Y * Z)
    def _(i):
        core_sum[i] = term[i, :, core] + core_in[i]

    copy = remote(core_sum.at[:, 1 - x_hi], x_in, 11, me + 2 - 4 * x_hi)
    copy.start()
    swap_w.wait()
    swap_att.wait()

    @pl.loop(0, tokens // TILE)
    def _(i):
        part = pl.ds(pl.multiple_of(i * TILE, TILE), TILE)
        total = dot(att[part, :], w_ref[:, mine_c]) + dot(att_other[part, :], w_other[...])
        out_ref[part, :] = total.astype(BF16)

    copy.wait()

    @pl.loop(0, Y * Z)
    def _(i):
        x_sum[i] = core_sum[i, x_hi] + x_in[i]

    for i in range(1, Y):
        to = lax.rem(y + i, Y)
        remote(x_sum.at[pl.ds(to * Z, Z)], y_in.at[y], 12, seq_at(to, z, x_hi, core)).start()
    y_in[y] = x_sum[pl.ds(y * Z, Z)]
    everyone = remote(y_in.at[pl.ds(0, Y - 1)], y_in.at[pl.ds(0, Y - 1)], 12, seq_at(lax.rem(y + 1, Y), z, x_hi, core))
    everyone.wait_send()
    everyone.wait_recv()
    y_sum[...] = y_in[0] + y_in[1] + y_in[2] + y_in[3]
    for i in range(1, Z):
        to = lax.rem(z + i, Z)
        remote(y_sum.at[to], z_in.at[z], 13, seq_at(y, to, x_hi, core)).start()
    z_in[z] = y_sum[z]
    everyone = remote(z_in.at[pl.ds(0, Z - 1)], z_in.at[pl.ds(0, Z - 1)], 13, seq_at(y, lax.rem(z + 1, Z), x_hi, core))
    everyone.wait_send()
    everyone.wait_recv()
    total = z_in[0]
    for i in range(1, Z):
        total = total + z_in[i]
    proj_ref[...] = (total * (1.0 / math.sqrt(tokens * SEQ))).T

    @pl.when(me > 0)
    def _():
        rim_back.wait_send()

    @pl.when(me < SEQ - 1)
    def _():
        rim_back.wait_recv()

    for t, (ref, sums) in enumerate(((dk_ref, dk_sum), (dv_ref, dv_sum))):
        for pair in range(2):
            lanes = slice(pair * 128, pair * 128 + 128)
            ref[:STRIDE, lanes] = sums[pair, STRIDE:tokens, :].astype(BF16)
            ref[STRIDE:, lanes] = (sums[pair, tokens:, :] + rim_recv[t, :, lanes].astype(F32)).astype(BF16)
    wait_all(res_grad, got_grad, 8)
    for t, ref in enumerate((dq_ref, dk_ref, dv_ref)):
        for hp in range(2):
            lanes = slice(half + hp * 128, half + hp * 128 + 128)
            ref[:, lanes] = from_messages(got_grad[hp * 64 : hp * 64 + 64, 16 * t : 16 * t + 16, :])


def local(queries, key_rows, value_rows, out_proj, grad_out, band_blocks, column_reach):
    tokens, width = queries.shape
    half = width // 2
    low = lambda *shape: pltpu.VMEM(shape, BF16)
    full = lambda *shape: pltpu.VMEM(shape, F32)
    vmem, smem = pl.BlockSpec(memory_space=pltpu.VMEM), pl.BlockSpec(memory_space=pltpu.SMEM)
    result = jax.ShapeDtypeStruct((tokens, width), BF16)
    return pl.pallas_call(
        layer_kernel,
        out_shape=(result, result, result, result, jax.ShapeDtypeStruct((width, 2 * width // SEQ), F32)),
        in_specs=[vmem] * 5 + [smem] * 2,
        out_specs=(vmem,) * 5,
        scratch_shapes=[
            low(SEQ, 48, 128), low(SEQ, 48, 128), low(SEQ, 16, 128), low(SEQ, 16, 128), full(SEQ, 1, 128),
            low(tokens, width), low(width, width), low(2, tokens + STRIDE, half), low(2, STRIDE, half),
            low(2, STRIDE, half),
            low(tokens, width), low(2 * width, tokens), full(2, tokens + STRIDE, 128), full(2, tokens + STRIDE, 128),
            full(4, 16 * SEQ, 128), full(4, 16 * SEQ, 128),
            low(SEQ, 16, 128), low(SEQ, 48, 128), low(SEQ, 16, 128), low(SEQ, 48, 128), low(tokens, width),
            low(tokens, width),
            full(Y * Z, XH, CORES, 8, width), full(Y * Z, XH, 8, width), full(Y * Z, XH, 8, width),
            full(Y * Z, 8, width), full(Y * Z, 8, width), full(Y, Z, 8, width), full(Z, 8, width), full(Z, 8, width),
            pltpu.SemaphoreType.DMA((14,)), pltpu.SemaphoreType.DMA((14,)),
        ],
        compiler_params=pltpu.CompilerParams(
            collective_id=0, has_side_effects=True, vmem_limit_bytes=60 * 2**20
        ),
        cost_estimate=pl.CostEstimate(flops=2 * 10**10, bytes_accessed=10 * 2**20, transcendentals=0),
    )(queries, key_rows, value_rows, out_proj, grad_out, band_blocks, column_reach)


def solution(mesh):
    tokens = P("seq", "head")
    return jax.shard_map(
        local,
        mesh=mesh,
        in_specs=(tokens, tokens, tokens, P("head", None), tokens, P("seq"), P("seq")),
        out_specs=(tokens, tokens, tokens, tokens, P("head", "seq")),
        check_vma=False,
    )
```

```python
import math

import jax
import jax.numpy as jnp
from jax import lax
from jax.experimental import pallas as pl
from jax.experimental.pallas import tpu as pltpu
from jax.sharding import PartitionSpec as P

HEAD_DIM = 64
STRIDE = 512
BLOCK = 64
TILE = 256
MASKED = -1e30
F32 = jnp.float32
BF16 = jnp.bfloat16
MESH = pl.DeviceIdType.MESH
Y, Z, XH, CORES = 4, 8, 2, 2
SEQ = Y * Z * XH * CORES


def dot(a, b):
    return jnp.dot(a, b, preferred_element_type=F32)


def turned(m):
    return m.astype(F32).T.astype(BF16)


def scaled(q):
    return (q.astype(F32) * HEAD_DIM**-0.5).astype(BF16)


def head_rows(h):
    return slice(h * HEAD_DIM, (h + 1) * HEAD_DIM)


def alone(m_t, h):
    blank = jnp.zeros((HEAD_DIM, m_t.shape[1]), BF16)
    return jnp.concatenate([m_t[head_rows(h)], blank] if h == 0 else [blank, m_t[head_rows(h)]], axis=0)


def pair_scores(q_t, k, allowed, h):
    return jnp.where(allowed, dot(k, alone(q_t, h)), MASKED)


def pair_forward(q, k, v, allowed):
    q_t, v_t = turned(scaled(q)), turned(v)
    outs, all_weights, stats = [], [], []
    for h in range(2):
        scores = pair_scores(q_t, k, allowed, h)
        highest = jnp.max(scores, axis=0, keepdims=True)
        weights = jnp.exp(scores - highest)
        share = 1.0 / jnp.sum(weights, axis=0, keepdims=True)
        weights = weights * share
        outs.append(dot(v_t[head_rows(h)], weights.astype(BF16)).astype(BF16).astype(F32))
        all_weights.append(weights)
        stats.append((highest, share))
    return jnp.concatenate(outs, axis=0), all_weights, stats


def pair_backward(q, k, v, d, out_t, weights_of):
    qs = scaled(q)
    q_t, d_t, k_t = turned(qs), turned(d), turned(k)
    first = lax.broadcasted_iota(jnp.int32, q.shape, 1) < HEAD_DIM
    nothing = jnp.zeros_like(q)
    dqs, dk, dv = [], None, None
    for h in range(2):
        mine = head_rows(h)
        weights = weights_of(h, q_t)
        delta = jnp.sum(out_t[mine] * d_t[mine].astype(F32), axis=0, keepdims=True)
        d_scores = (weights * (dot(v, alone(d_t, h)) - delta)).astype(BF16)
        dqs.append(dot(k_t[mine], d_scores) * HEAD_DIM**-0.5)
        keep = first if h == 0 else jnp.logical_not(first)
        dk_h = dot(d_scores, jnp.where(keep, qs, nothing))
        dv_h = dot(weights.astype(BF16), jnp.where(keep, d, nothing))
        dk = dk_h if dk is None else dk + dk_h
        dv = dv_h if dv is None else dv + dv_h
    return jnp.concatenate(dqs, axis=0).T, dk, dv


def dot_nt(a, b):
    return lax.dot_general(a, b, (((1,), (1,)), ((), ())), preferred_element_type=F32)


def row_of(count, part, values):
    run = lax.broadcasted_iota(jnp.int32, (1, count), 1) // part
    row = jnp.zeros((1, count), jnp.int32)
    for i, value in enumerate(values):
        row = jnp.where(run == i, value, row)
    return row


def to_messages(x):
    grid = x.astype(F32).reshape(2, STRIDE // 8, 8, 128)
    return jnp.concatenate([grid[0], grid[1]], axis=1).astype(BF16)


def from_messages(m):
    grid = m.astype(F32)
    halves = [grid[:, 8 * r : 8 * r + 8].reshape(STRIDE, 128) for r in range(2)]
    return jnp.concatenate(halves, axis=0).astype(BF16)


def layer_kernel(
    q_in, k_in, v_in, w_in, g_in, band_ref, reach_ref,
    out_to, dq_to, dk_to, dv_to, got_grad, proj_ref,
    q_ref, k_ref, v_ref, w_ref, g_ref, out_ref, dq_ref, dk_ref, dv_ref,
    qkv_send, qkv_recv, col_d_send, col_d_recv, reach_all,
    g_other, w_other, rim, rim_send, rim_recv,
    d_att, g_t, dk_sum, dv_sum, stats, wide, back, col_weights, col_out_t,
    res_out, res_grad, got_out, att, att_other,
    term, core_in, core_sum, y_in, y_sum, x_in, x_sum, z_in,
    send, recv, near,
):
    tokens, width = q_ref.shape
    half = width // 2
    me, head = lax.axis_index("seq"), lax.axis_index("head")
    core, x_hi, z, y = lax.rem(me, 2), lax.rem(me // 2, 2), lax.rem(me // 4, Z), me // (4 * Z)

    def seq_at(y, z, x_hi, core):
        return ((y * Z + z) * XH + x_hi) * CORES + core

    def remote(src, dst, n, seq, other=None):
        return pltpu.make_async_remote_copy(
            src_ref=src, dst_ref=dst, send_sem=send.at[n], recv_sem=recv.at[n],
            device_id=(seq, head if other is None else other), device_id_type=MESH,
        )

    def exchange(start):
        place = (me // 4) * 2 + core

        def peer(i, side):
            to = lax.rem(place + i, SEQ // 2)
            return (to // 2) * 4 + side * 2 + lax.rem(to, 2)

        @pl.loop(1, SEQ // 2)
        def _(i):
            start(peer(i, x_hi))

        @pl.loop(0, SEQ // 2)
        def _(i):
            start(peer(i, 1 - x_hi))

    def wait_all(src, dst, n):
        everyone = remote(src.at[pl.ds(0, SEQ - 1)], dst.at[pl.ds(0, SEQ - 1)], n, lax.rem(me + 1, SEQ))
        everyone.wait_send()
        everyone.wait_recv()

    loads = [
        pltpu.make_async_copy(a, b, near.at[i])
        for i, (a, b) in enumerate(((k_in, k_ref), (v_in, v_ref), (q_in, q_ref), (g_in, g_ref), (w_in, w_ref)))
    ]
    for load in loads:
        load.start()

    def store(n, src, dst):
        copy = pltpu.make_async_copy(src, dst, near.at[len(loads) + n])
        copy.start()
        return copy

    barrier = pltpu.get_barrier_semaphore()
    pl.semaphore_signal(barrier, inc=1, device_id=(me, 1 - head), device_id_type=MESH)

    @pl.loop(1, SEQ)
    def _(i):
        pl.semaphore_signal(barrier, inc=1, device_id=(lax.rem(me + i, SEQ), head), device_id_type=MESH)

    reach_all[me] = row_of(128, 1, [reach_ref[i] for i in range(16)]).astype(F32)
    for load in loads:
        load.wait()
    for t, ref in enumerate((q_ref, k_ref, v_ref)):
        for hp in range(2):
            lanes = slice(half + hp * 128, half + hp * 128 + 128)
            qkv_send[hp * 64 : hp * 64 + 64, 16 * t : 16 * t + 16, :] = to_messages(ref[:, lanes])
    for t, ref in enumerate((k_ref, v_ref)):
        rim[t, STRIDE:, :] = ref[:, :half]
    pl.semaphore_wait(barrier, SEQ)

    swap_g = remote(g_ref, g_other, 0, me, 1 - head)
    swap_g.start()

    rim_to = remote(rim.at[:, pl.ds(tokens, STRIDE)], rim.at[:, pl.ds(0, STRIDE)], 4, jnp.minimum(me + 1, SEQ - 1))

    @pl.when(me < SEQ - 1)
    def _():
        rim_to.start()

    @pl.when(me == 0)
    def _():
        rim[:, :STRIDE, :] = jnp.zeros((2, STRIDE, half), BF16)

    def start(to):
        remote(qkv_send.at[to], qkv_recv.at[me], 2, to).start()
        remote(reach_all.at[me], reach_all.at[me], 3, to).start()

    exchange(start)
    qkv_recv[me] = qkv_send[me]

    mine_c = pl.ds(pl.multiple_of(head * width, 128), width)
    other_c = pl.ds(pl.multiple_of((1 - head) * width, 128), width)

    def turn(ref, rows):
        for i in range(tokens // TILE):
            part = slice(i * TILE, i * TILE + TILE)
            g_t[rows, part] = turned(ref[part, :])

    turn(g_ref, mine_c)

    @pl.when(me < SEQ - 1)
    def _():
        rim_to.wait_send()

    @pl.when(me > 0)
    def _():
        rim_to.wait_recv()

    span = TILE + STRIDE
    edge = jnp.where(me == 0, STRIDE, 0)

    def band_step(step):
        begin = pl.multiple_of(step * TILE, TILE)
        key_at = lax.broadcasted_iota(jnp.int32, (span, TILE), 0)
        query_at = STRIDE + lax.broadcasted_iota(jnp.int32, (span, TILE), 1)
        count = row_of(TILE, BLOCK, [band_ref[step * (TILE // BLOCK) + i] for i in range(TILE // BLOCK)])
        lowest = jnp.maximum((query_at[:1] // BLOCK - count + 1) * BLOCK, edge - begin)
        return pl.ds(begin, TILE), pl.ds(begin, span), (key_at <= query_at) & (key_at >= lowest)

    pairs = [slice(pair * 128, pair * 128 + 128) for pair in range(2)]

    @pl.loop(0, tokens // TILE)
    def _(step):
        mine, span_at, allowed = band_step(step)
        for pair, lanes in enumerate(pairs):
            out_t, _, rows = pair_forward(q_ref[mine, lanes], rim[0, span_at, lanes], rim[1, span_at, lanes], allowed)
            att[mine, lanes] = out_t.T.astype(BF16)
            stats[step, 4 * pair : 4 * pair + 4, :] = jnp.concatenate([*rows[0], *rows[1]], axis=0)

    swap_g.wait()

    @pl.loop(0, tokens // TILE)
    def _(i):
        part = pl.ds(pl.multiple_of(i * TILE, TILE), TILE)
        d = dot_nt(g_ref[part, :], w_ref[:, mine_c]) + dot_nt(g_other[part, :], w_ref[:, other_c])
        d_att[part, :] = d.astype(BF16)

    for hp in range(2):
        lanes = slice(half + hp * 128, half + hp * 128 + 128)
        col_d_send[hp * 64 : hp * 64 + 64] = to_messages(d_att[:, lanes])
    exchange(lambda to: remote(col_d_send.at[to], col_d_recv.at[me], 5, to).start())
    col_d_recv[me] = col_d_send[me]

    part_w = pl.ds(pl.multiple_of(core * (width // 2), 16), width // 2)
    swap_w = remote(w_ref.at[part_w, other_c], w_other.at[part_w], 1, me, 1 - head)
    swap_w.start()
    share_w = remote(w_other.at[part_w], w_other.at[part_w], 6, me + 1 - 2 * core)
    swap_band = remote(att.at[:, pl.ds(0, half)], att_other.at[:, pl.ds(0, half)], 9, me, 1 - head)
    swap_band.start()
    turn(g_other, other_c)

    def sum_core(n):
        @pl.loop(0, Y)
        def _(i):
            part = pl.ds(pl.multiple_of(i * TILE, TILE), TILE)
            term[n, i] = dot(g_t[part, :], att[:, n * half : n * half + half]).reshape(Z, XH, CORES, 8, half)

        copy = remote(term.at[n, :, :, :, 1 - core], core_in.at[n], 10 + 4 * n, me + 1 - 2 * core)
        copy.start()
        return copy

    def sum_y(n, copy):
        copy.wait()

        @pl.loop(0, Y)
        def _(i):
            core_sum[n, i] = term[n, i, :, :, core] + core_in[n, i]

        for i in range(1, Y):
            to = lax.rem(y + i, Y)
            remote(core_sum.at[n, to], y_in.at[n, y], 11 + 4 * n, seq_at(to, z, x_hi, core)).start()
        y_in[n, y] = core_sum[n, y]
        some = y_in.at[n, pl.ds(0, Y - 1)]
        return remote(some, some, 11 + 4 * n, seq_at(lax.rem(y + 1, Y), z, x_hi, core))

    def sum_x(n, copy):
        copy.wait_send()
        copy.wait_recv()
        y_sum[n] = y_in[n, 0] + y_in[n, 1] + y_in[n, 2] + y_in[n, 3]
        copy = remote(y_sum.at[n, :, 1 - x_hi], x_in.at[n], 12 + 4 * n, me + 2 - 4 * x_hi)
        copy.start()
        return copy

    def sum_z(n, copy):
        copy.wait()
        x_sum[n] = y_sum[n, :, x_hi] + x_in[n]
        for i in range(1, Z):
            to = lax.rem(z + i, Z)
            remote(x_sum.at[n, to], z_in.at[n, z], 13 + 4 * n, seq_at(y, to, x_hi, core)).start()
        z_in[n, z] = x_sum[n, z]
        some = z_in.at[n, pl.ds(0, Z - 1)]
        return remote(some, some, 13 + 4 * n, seq_at(y, lax.rem(z + 1, Z), x_hi, core))

    def sum_end(n, copy):
        copy.wait_send()
        copy.wait_recv()
        total = z_in[n, 0]
        for i in range(1, Z):
            total = total + z_in[n, i]
        proj_ref[:, n * half : n * half + half] = total * (1.0 / math.sqrt(tokens * SEQ))

    band_sum = sum_core(0)

    wait_all(reach_all, reach_all, 3)
    wait_all(qkv_send, qkv_recv, 2)
    for t in range(3):
        wide[t] = qkv_recv[:, 16 * t : 16 * t + 16, :].astype(F32).reshape(16 * SEQ, 128)
    table = reach_all[...].reshape(SEQ, 128).T
    block = lax.rem(me, 64) // 8
    row_at = lax.broadcasted_iota(jnp.int32, (128, SEQ), 0)
    reach = jnp.concatenate(
        [jnp.sum(jnp.where(row_at == block + 8 * r, table, 0.0), axis=0, keepdims=True) for r in range(2)], axis=1
    ).astype(jnp.int32)
    rows = 2 * SEQ

    def image_row(axis):
        i = lax.broadcasted_iota(jnp.int32, (rows, rows), axis)
        return 2 * lax.rem(i, SEQ) + i // SEQ

    def column_rows(column):
        return [pl.ds(column + 8 * r, SEQ, stride=16) for r in range(2)]

    def column_of(ts, column):
        at = column_rows(column)
        return [jnp.concatenate([wide[t, at[0], :], wide[t, at[1], :]], axis=0).astype(BF16) for t in ts]

    @pl.loop(0, 8)
    def _(column):
        apart = image_row(1) - image_row(0)
        allowed = (apart >= 0) & (apart < reach)
        out_t, weights, _ = pair_forward(*column_of(range(3), column), allowed)
        col_out_t[column] = out_t
        for h in range(2):
            col_weights[column, h] = weights[h]
        out = out_t.T
        for r, at in enumerate(column_rows(column)):
            back[at, :] = out[r * SEQ : r * SEQ + SEQ]

    res_out[...] = back[...].reshape(SEQ, 16, 128).astype(BF16)
    exchange(lambda to: remote(res_out.at[to], got_out.at[me], 7, to).start())
    got_out[me] = res_out[me]
    band_sum = sum_y(0, band_sum)
    swap_w.wait()
    share_w.start()

    wait_all(col_d_send, col_d_recv, 5)
    wide[3] = col_d_recv[...].astype(F32).reshape(16 * SEQ, 128)

    @pl.loop(0, 8)
    def _(column):
        values = pair_backward(
            *column_of(range(4), column), col_out_t[column], lambda h, q_t: col_weights[column, h]
        )
        for t, value in enumerate(values):
            for r, at in enumerate(column_rows(column)):
                wide[t, at, :] = value[r * SEQ : r * SEQ + SEQ]

    for t in range(3):
        res_grad[:, 16 * t : 16 * t + 16, :] = wide[t].reshape(SEQ, 16, 128).astype(BF16)
    exchange(lambda to: remote(res_grad.at[to], got_grad.at[me], 8, to).start())
    stores = [store(0, res_grad.at[me], got_grad.at[me])]
    band_sum = sum_x(0, band_sum)

    wait_all(res_out, got_out, 7)
    for hp in range(2):
        att[:, half + hp * 128 : half + hp * 128 + 128] = from_messages(got_out[hp * 64 : hp * 64 + 64])
    swap_column = remote(att.at[:, pl.ds(half, half)], att_other.at[:, pl.ds(half, half)], 18, me, 1 - head)
    swap_column.start()
    column_sum = sum_core(1)

    for pair in range(2):
        dk_sum[pair] = jnp.zeros((tokens + STRIDE, 128), F32)
        dv_sum[pair] = jnp.zeros((tokens + STRIDE, 128), F32)

    def band_backward(step):
        mine, span_at, allowed = band_step(step)
        for pair, lanes in enumerate(pairs):
            k = rim[0, span_at, lanes]

            def weights_of(h, q_t):
                at = 4 * pair + 2 * h
                highest, share = stats[step, at : at + 1, :], stats[step, at + 1 : at + 2, :]
                return jnp.exp(pair_scores(q_t, k, allowed, h) - highest) * share

            dq, dk, dv = pair_backward(
                q_ref[mine, lanes], k, rim[1, span_at, lanes], d_att[mine, lanes],
                att[mine, lanes].astype(F32).T, weights_of,
            )
            dq_ref[mine, lanes] = dq.astype(BF16)
            dk_sum[pair, span_at, :] += dk
            dv_sum[pair, span_at, :] += dv

    pl.loop(0, 2)(band_backward)
    for pair, lanes in enumerate(pairs):
        rim_send[0, :, lanes] = dk_sum[pair, :STRIDE, :].astype(BF16)
        rim_send[1, :, lanes] = dv_sum[pair, :STRIDE, :].astype(BF16)
    rim_back = remote(rim_send, rim_recv, 19, jnp.maximum(me - 1, 0))

    @pl.when(me > 0)
    def _():
        rim_back.start()

    @pl.when(me == SEQ - 1)
    def _():
        rim_recv[...] = jnp.zeros((2, STRIDE, half), BF16)

    column_sum = sum_y(1, column_sum)
    band_sum = sum_z(0, band_sum)
    pl.loop(2, tokens // TILE)(band_backward)
    column_sum = sum_x(1, column_sum)
    sum_end(0, band_sum)
    share_w.wait()
    swap_band.wait()
    swap_column.wait()

    @pl.loop(0, tokens // TILE)
    def _(i):
        part = pl.ds(pl.multiple_of(i * TILE, TILE), TILE)
        total = dot(att[part, :], w_ref[:, mine_c]) + dot(att_other[part, :], w_other[...])
        out_ref[part, :] = total.astype(BF16)

    stores.append(store(1, out_ref, out_to))
    stores.append(store(2, dq_ref, dq_to))
    column_sum = sum_z(1, column_sum)

    @pl.when(me > 0)
    def _():
        rim_back.wait_send()

    @pl.when(me < SEQ - 1)
    def _():
        rim_back.wait_recv()

    for t, (ref, sums) in enumerate(((dk_ref, dk_sum), (dv_ref, dv_sum))):
        for pair, lanes in enumerate(pairs):
            ref[:STRIDE, lanes] = sums[pair, STRIDE:tokens, :].astype(BF16)
            ref[STRIDE:, lanes] = (sums[pair, tokens:, :] + rim_recv[t, :, lanes].astype(F32)).astype(BF16)
    stores.append(store(3, dk_ref, dk_to))
    stores.append(store(4, dv_ref, dv_to))
    sum_end(1, column_sum)
    for copy in stores:
        copy.wait()
    wait_all(res_grad, got_grad, 8)


def result_kernel(out_ref, dq_ref, dk_ref, dv_ref, got_ref, out, dq, dk, dv, got, whole, sem):
    half = dq_ref.shape[1]
    loads, stores = [], []
    for t, band in enumerate((dq_ref, dk_ref, dv_ref)):
        part = pl.ds(16 * t, 16)
        loads.append(pltpu.make_async_copy(got_ref.at[:, part], got.at[:, part], sem.at[2 * t]))
        loads.append(pltpu.make_async_copy(band, whole.at[t, :, pl.ds(0, half)], sem.at[2 * t + 1]))
    loads.append(pltpu.make_async_copy(out_ref, whole.at[3], sem.at[6]))
    for load in loads:
        load.start()
    for t, result in enumerate((dq, dk, dv)):
        loads[2 * t].wait()
        for hp in range(2):
            lanes = slice(half + hp * 128, half + hp * 128 + 128)
            whole[t, :, lanes] = from_messages(got[hp * 64 : hp * 64 + 64, 16 * t : 16 * t + 16, :])
        loads[2 * t + 1].wait()
        stores.append(pltpu.make_async_copy(whole.at[t], result, sem.at[7 + t]))
        stores[-1].start()
    loads[6].wait()
    stores.append(pltpu.make_async_copy(whole.at[3], out, sem.at[10]))
    stores[-1].start()
    for store in stores:
        store.wait()


def local(queries, key_rows, value_rows, out_proj, grad_out, band_blocks, column_reach):
    tokens, width = queries.shape
    half = width // 2
    low = lambda *shape: pltpu.VMEM(shape, BF16)
    full = lambda *shape: pltpu.VMEM(shape, F32)
    vmem, smem = pl.BlockSpec(memory_space=pltpu.VMEM), pl.BlockSpec(memory_space=pltpu.SMEM)
    any_place = pl.BlockSpec(memory_space=pl.ANY)
    shape = jax.ShapeDtypeStruct
    result, banded = shape((tokens, width), BF16), shape((tokens, half), BF16)
    *parts, proj_grad = pl.pallas_call(
        layer_kernel,
        out_shape=(result, banded, banded, banded, shape((SEQ, 48, 128), BF16), shape((2 * width // SEQ, width), F32)),
        in_specs=[any_place] * 5 + [smem] * 2,
        out_specs=(any_place,) * 5 + (vmem,),
        scratch_shapes=[
            low(tokens, width), low(tokens, width), low(tokens, width), low(width, 2 * width), low(tokens, width),
            low(tokens, width), low(tokens, half), low(tokens, half), low(tokens, half),
            low(SEQ, 48, 128), low(SEQ, 48, 128), low(SEQ, 16, 128), low(SEQ, 16, 128), full(SEQ, 1, 128),
            low(tokens, width), low(width, width), low(2, tokens + STRIDE, half), low(2, STRIDE, half),
            low(2, STRIDE, half),
            low(tokens, width), low(2 * width, tokens), full(2, tokens + STRIDE, 128), full(2, tokens + STRIDE, 128),
            full(tokens // TILE, 8, TILE), full(4, 16 * SEQ, 128), full(16 * SEQ, 128), full(8, 2, 2 * SEQ, 2 * SEQ),
            full(8, 128, 2 * SEQ),
            low(SEQ, 16, 128), low(SEQ, 48, 128), low(SEQ, 16, 128), low(tokens, width), low(tokens, width),
            full(2, Y, Z, XH, CORES, 8, half), full(2, Y, Z, XH, 8, half), full(2, Y, Z, XH, 8, half),
            full(2, Y, Z, XH, 8, half), full(2, Z, XH, 8, half), full(2, Z, 8, half), full(2, Z, 8, half),
            full(2, Z, 8, half),
            pltpu.SemaphoreType.DMA((20,)), pltpu.SemaphoreType.DMA((20,)), pltpu.SemaphoreType.DMA((10,)),
        ],
        compiler_params=pltpu.CompilerParams(
            collective_id=0, has_side_effects=True, vmem_limit_bytes=56 * 2**20
        ),
        cost_estimate=pl.CostEstimate(flops=2 * 10**10, bytes_accessed=10 * 2**20, transcendentals=0),
    )(queries, key_rows, value_rows, out_proj, grad_out, band_blocks, column_reach)
    grads = pl.pallas_call(
        result_kernel,
        out_shape=(result,) * 4,
        in_specs=[any_place] * 5,
        out_specs=(any_place,) * 4,
        scratch_shapes=[low(SEQ, 48, 128), low(4, tokens, width), pltpu.SemaphoreType.DMA((11,))],
        compiler_params=pltpu.CompilerParams(vmem_limit_bytes=56 * 2**20),
        cost_estimate=pl.CostEstimate(flops=0, bytes_accessed=8 * 2**20, transcendentals=0),
    )(*parts)
    return (*grads, proj_grad.T)


def solution(mesh):
    tokens = P("seq", "head")
    return jax.shard_map(
        local,
        mesh=mesh,
        in_specs=(tokens, tokens, tokens, P("head", None), tokens, P("seq"), P("seq")),
        out_specs=(tokens, tokens, tokens, tokens, P("head", "seq")),
        check_vma=False,
    )
```

```python
import math

import jax
import jax.numpy as jnp
from jax import lax
from jax.experimental import pallas as pl
from jax.experimental.pallas import tpu as pltpu
from jax.sharding import PartitionSpec as P

HEAD_DIM = 64
STRIDE = 512
BLOCK = 64
TILE = 256
MASKED = -1e30
F32 = jnp.float32
BF16 = jnp.bfloat16
MESH = pl.DeviceIdType.MESH
Y, Z, XH, CORES = 4, 8, 2, 2
SEQ = Y * Z * XH * CORES


def dot(a, b):
    return jnp.dot(a, b, preferred_element_type=F32)


def turned(m):
    return m.astype(F32).T.astype(BF16)


def scaled(q):
    return (q.astype(F32) * HEAD_DIM**-0.5).astype(BF16)


def head_rows(h):
    return slice(h * HEAD_DIM, (h + 1) * HEAD_DIM)


def alone(m_t, h):
    blank = jnp.zeros((HEAD_DIM, m_t.shape[1]), BF16)
    return jnp.concatenate([m_t[head_rows(h)], blank] if h == 0 else [blank, m_t[head_rows(h)]], axis=0)


def pair_scores(q_t, k, allowed, h):
    return jnp.where(allowed, dot(k, alone(q_t, h)), MASKED)


def pair_forward(q, k, v, allowed):
    q_t, v_t = turned(scaled(q)), turned(v)
    outs, all_weights, stats = [], [], []
    for h in range(2):
        scores = pair_scores(q_t, k, allowed, h)
        highest = jnp.max(scores, axis=0, keepdims=True)
        weights = jnp.exp(scores - highest)
        share = 1.0 / jnp.sum(weights, axis=0, keepdims=True)
        weights = weights * share
        outs.append(dot(v_t[head_rows(h)], weights.astype(BF16)).astype(BF16).astype(F32))
        all_weights.append(weights)
        stats.append((highest, share))
    return jnp.concatenate(outs, axis=0), all_weights, stats


def pair_backward(q, k, v, d, out_t, weights_of):
    qs = scaled(q)
    q_t, d_t, k_t = turned(qs), turned(d), turned(k)
    first = lax.broadcasted_iota(jnp.int32, q.shape, 1) < HEAD_DIM
    nothing = jnp.zeros_like(q)
    dqs, dk, dv = [], None, None
    for h in range(2):
        mine = head_rows(h)
        weights = weights_of(h, q_t)
        delta = jnp.sum(out_t[mine] * d_t[mine].astype(F32), axis=0, keepdims=True)
        d_scores = (weights * (dot(v, alone(d_t, h)) - delta)).astype(BF16)
        dqs.append(dot(k_t[mine], d_scores) * HEAD_DIM**-0.5)
        keep = first if h == 0 else jnp.logical_not(first)
        dk_h = dot(d_scores, jnp.where(keep, qs, nothing))
        dv_h = dot(weights.astype(BF16), jnp.where(keep, d, nothing))
        dk = dk_h if dk is None else dk + dk_h
        dv = dv_h if dv is None else dv + dv_h
    return jnp.concatenate(dqs, axis=0).T, dk, dv


def dot_nt(a, b):
    return lax.dot_general(a, b, (((1,), (1,)), ((), ())), preferred_element_type=F32)


def row_of(count, part, values):
    run = lax.broadcasted_iota(jnp.int32, (1, count), 1) // part
    row = jnp.zeros((1, count), jnp.int32)
    for i, value in enumerate(values):
        row = jnp.where(run == i, value, row)
    return row


def to_messages(x):
    grid = x.astype(F32).reshape(2, STRIDE // 8, 8, 128)
    return jnp.concatenate([grid[0], grid[1]], axis=1).astype(BF16)


def from_messages(m):
    grid = m.astype(F32)
    halves = [grid[:, 8 * r : 8 * r + 8].reshape(STRIDE, 128) for r in range(2)]
    return jnp.concatenate(halves, axis=0).astype(BF16)


def layer_kernel(
    q_in, k_in, v_in, w_in, g_in, band_ref, reach_ref,
    out_to, dq_to, dk_to, dv_to, got_grad, proj_ref,
    q_ref, k_ref, v_ref, w_ref, g_ref, out_ref, dq_ref, dk_ref, dv_ref,
    qkv_send, qkv_recv, col_d_send, col_d_recv, reach_all,
    g_other, w_other, rim, rim_send, rim_recv,
    d_att, g_t, dk_sum, dv_sum, stats, wide, back, col_weights, col_out_t,
    res_out, res_grad, got_out, att, att_other,
    term, core_in, core_sum, y_in, y_sum, x_in, x_sum, z_in,
    send, recv, near,
):
    tokens, width = q_ref.shape
    half = width // 2
    me, head = lax.axis_index("seq"), lax.axis_index("head")
    core, x_hi, z, y = lax.rem(me, 2), lax.rem(me // 2, 2), lax.rem(me // 4, Z), me // (4 * Z)

    def seq_at(y, z, x_hi, core):
        return ((y * Z + z) * XH + x_hi) * CORES + core

    def remote(src, dst, n, seq, other=None):
        return pltpu.make_async_remote_copy(
            src_ref=src, dst_ref=dst, send_sem=send.at[n], recv_sem=recv.at[n],
            device_id=(seq, head if other is None else other), device_id_type=MESH,
        )

    place = (me // 4) * 2 + core

    def peer(i, side):
        to = lax.rem(place + i, SEQ // 2)
        return (to // 2) * 4 + side * 2 + lax.rem(to, 2)

    def exchange_near(start):
        @pl.loop(1, SEQ // 2, unroll=7)
        def _(i):
            start(peer(i, x_hi))

    def exchange_far(start):
        @pl.loop(0, SEQ // 2, unroll=8)
        def _(i):
            start(peer(i, 1 - x_hi))

    def exchange(start):
        exchange_near(start)
        exchange_far(start)

    def wait_all(src, dst, n):
        everyone = remote(src.at[pl.ds(0, SEQ - 1)], dst.at[pl.ds(0, SEQ - 1)], n, lax.rem(me + 1, SEQ))
        everyone.wait_send()
        everyone.wait_recv()

    loads = [
        pltpu.make_async_copy(a, b, near.at[i])
        for i, (a, b) in enumerate(((k_in, k_ref), (v_in, v_ref), (q_in, q_ref), (g_in, g_ref), (w_in, w_ref)))
    ]
    for load in loads:
        load.start()

    def store(n, src, dst):
        copy = pltpu.make_async_copy(src, dst, near.at[len(loads) + n])
        copy.start()
        return copy

    barrier = pltpu.get_barrier_semaphore()
    pl.semaphore_signal(barrier, inc=1, device_id=(me, 1 - head), device_id_type=MESH)

    @pl.loop(1, SEQ)
    def _(i):
        pl.semaphore_signal(barrier, inc=1, device_id=(lax.rem(me + i, SEQ), head), device_id_type=MESH)

    reach_all[me] = row_of(128, 1, [reach_ref[i] for i in range(16)]).astype(F32)
    for load in loads:
        load.wait()
    for t, ref in enumerate((q_ref, k_ref, v_ref)):
        for hp in range(2):
            lanes = slice(half + hp * 128, half + hp * 128 + 128)
            qkv_send[hp * 64 : hp * 64 + 64, 16 * t : 16 * t + 16, :] = to_messages(ref[:, lanes])
    for t, ref in enumerate((k_ref, v_ref)):
        rim[t, STRIDE:, :] = ref[:, :half]
    pl.semaphore_wait(barrier, SEQ)

    swap_g = remote(g_ref, g_other, 0, me, 1 - head)
    swap_g.start()

    rim_to = remote(rim.at[:, pl.ds(tokens, STRIDE)], rim.at[:, pl.ds(0, STRIDE)], 4, jnp.minimum(me + 1, SEQ - 1))

    @pl.when(me < SEQ - 1)
    def _():
        rim_to.start()

    @pl.when(me == 0)
    def _():
        rim[:, :STRIDE, :] = jnp.zeros((2, STRIDE, half), BF16)

    reach_core = remote(reach_all.at[me], reach_all.at[me], 3, me + 1 - 2 * core)
    reach_core.start()

    def send_qkv(to):
        remote(qkv_send.at[to], qkv_recv.at[me], 2, to).start()

    exchange_near(send_qkv)
    qkv_recv[me] = qkv_send[me]
    reach_core.wait()
    two = pl.ds(me - core, 2)
    reach_x = remote(reach_all.at[two], reach_all.at[two], 20, me + 2 - 4 * x_hi)
    reach_x.start()

    mine_c = pl.ds(pl.multiple_of(head * width, 128), width)
    other_c = pl.ds(pl.multiple_of((1 - head) * width, 128), width)

    def turn(ref, rows):
        for i in range(tokens // TILE):
            part = slice(i * TILE, i * TILE + TILE)
            g_t[rows, part] = turned(ref[part, :])

    turn(g_ref, mine_c)

    @pl.when(me < SEQ - 1)
    def _():
        rim_to.wait_send()

    @pl.when(me > 0)
    def _():
        rim_to.wait_recv()

    span = TILE + STRIDE
    edge = jnp.where(me == 0, STRIDE, 0)

    def band_step(step):
        begin = pl.multiple_of(step * TILE, TILE)
        key_at = lax.broadcasted_iota(jnp.int32, (span, TILE), 0)
        query_at = STRIDE + lax.broadcasted_iota(jnp.int32, (span, TILE), 1)
        count = row_of(TILE, BLOCK, [band_ref[step * (TILE // BLOCK) + i] for i in range(TILE // BLOCK)])
        lowest = jnp.maximum((query_at[:1] // BLOCK - count + 1) * BLOCK, edge - begin)
        return pl.ds(begin, TILE), pl.ds(begin, span), (key_at <= query_at) & (key_at >= lowest)

    pairs = [slice(pair * 128, pair * 128 + 128) for pair in range(2)]

    @pl.loop(0, tokens // TILE)
    def _(step):
        mine, span_at, allowed = band_step(step)
        for pair, lanes in enumerate(pairs):
            out_t, _, rows = pair_forward(q_ref[mine, lanes], rim[0, span_at, lanes], rim[1, span_at, lanes], allowed)
            att[mine, lanes] = out_t.T.astype(BF16)
            stats[step, 4 * pair : 4 * pair + 4, :] = jnp.concatenate([*rows[0], *rows[1]], axis=0)

    exchange_far(send_qkv)
    reach_x.wait()
    four = pl.ds(me - core - 2 * x_hi, 4)
    for i in range(1, Z):
        to = seq_at(y, lax.rem(z + i, Z), x_hi, core)
        remote(reach_all.at[four], reach_all.at[four], 21, to).start()

    swap_g.wait()

    @pl.loop(0, tokens // TILE)
    def _(i):
        part = pl.ds(pl.multiple_of(i * TILE, TILE), TILE)
        d = dot_nt(g_ref[part, :], w_ref[:, mine_c]) + dot_nt(g_other[part, :], w_ref[:, other_c])
        d_att[part, :] = d.astype(BF16)

    for hp in range(2):
        lanes = slice(half + hp * 128, half + hp * 128 + 128)
        col_d_send[hp * 64 : hp * 64 + 64] = to_messages(d_att[:, lanes])
    exchange(lambda to: remote(col_d_send.at[to], col_d_recv.at[me], 5, to).start())
    col_d_recv[me] = col_d_send[me]

    some = reach_all.at[pl.ds(0, 4 * (Z - 1))]
    reach_z = remote(some, some, 21, seq_at(y, lax.rem(z + 1, Z), x_hi, core))
    reach_z.wait_send()
    reach_z.wait_recv()
    slab = pl.ds(y * (4 * Z), 4 * Z)
    for i in range(1, Y):
        to = seq_at(lax.rem(y + i, Y), z, x_hi, core)
        remote(reach_all.at[slab], reach_all.at[slab], 22, to).start()

    part_w = pl.ds(pl.multiple_of(core * (width // 2), 16), width // 2)
    swap_w = remote(w_ref.at[part_w, other_c], w_other.at[part_w], 1, me, 1 - head)
    swap_w.start()
    share_w = remote(w_other.at[part_w], w_other.at[part_w], 6, me + 1 - 2 * core)
    swap_band = remote(att.at[:, pl.ds(0, half)], att_other.at[:, pl.ds(0, half)], 9, me, 1 - head)
    swap_band.start()
    turn(g_other, other_c)

    def sum_core(n):
        @pl.loop(0, Y)
        def _(i):
            part = pl.ds(pl.multiple_of(i * TILE, TILE), TILE)
            term[n, i] = dot(g_t[part, :], att[:, n * half : n * half + half]).reshape(Z, XH, CORES, 8, half)

        copy = remote(term.at[n, :, :, :, 1 - core], core_in.at[n], 10 + 4 * n, me + 1 - 2 * core)
        copy.start()
        return copy

    def sum_y(n, copy):
        copy.wait()

        @pl.loop(0, Y)
        def _(i):
            core_sum[n, i] = term[n, i, :, :, core] + core_in[n, i]

        for i in range(1, Y):
            to = lax.rem(y + i, Y)
            remote(core_sum.at[n, to], y_in.at[n, y], 11 + 4 * n, seq_at(to, z, x_hi, core)).start()
        y_in[n, y] = core_sum[n, y]
        some = y_in.at[n, pl.ds(0, Y - 1)]
        return remote(some, some, 11 + 4 * n, seq_at(lax.rem(y + 1, Y), z, x_hi, core))

    def sum_x(n, copy):
        copy.wait_send()
        copy.wait_recv()
        y_sum[n] = y_in[n, 0] + y_in[n, 1] + y_in[n, 2] + y_in[n, 3]
        copy = remote(y_sum.at[n, :, 1 - x_hi], x_in.at[n], 12 + 4 * n, me + 2 - 4 * x_hi)
        copy.start()
        return copy

    def sum_z(n, copy):
        copy.wait()
        x_sum[n] = y_sum[n, :, x_hi] + x_in[n]
        for i in range(1, Z):
            to = lax.rem(z + i, Z)
            remote(x_sum.at[n, to], z_in.at[n, z], 13 + 4 * n, seq_at(y, to, x_hi, core)).start()
        z_in[n, z] = x_sum[n, z]
        some = z_in.at[n, pl.ds(0, Z - 1)]
        return remote(some, some, 13 + 4 * n, seq_at(y, lax.rem(z + 1, Z), x_hi, core))

    def sum_end(n, copy):
        copy.wait_send()
        copy.wait_recv()
        total = z_in[n, 0]
        for i in range(1, Z):
            total = total + z_in[n, i]
        proj_ref[:, n * half : n * half + half] = total * (1.0 / math.sqrt(tokens * SEQ))

    band_sum = sum_core(0)

    some = reach_all.at[pl.ds(0, 4 * Z * (Y - 1))]
    reach_y = remote(some, some, 22, seq_at(lax.rem(y + 1, Y), z, x_hi, core))
    reach_y.wait_send()
    reach_y.wait_recv()
    wait_all(qkv_send, qkv_recv, 2)
    for t in range(3):
        wide[t] = qkv_recv[:, 16 * t : 16 * t + 16, :].astype(F32).reshape(16 * SEQ, 128)
    table = reach_all[...].reshape(SEQ, 128).T
    block = lax.rem(me, 64) // 8
    row_at = lax.broadcasted_iota(jnp.int32, (128, SEQ), 0)
    reach = jnp.concatenate(
        [jnp.sum(jnp.where(row_at == block + 8 * r, table, 0.0), axis=0, keepdims=True) for r in range(2)], axis=1
    ).astype(jnp.int32)
    rows = 2 * SEQ

    def image_row(axis):
        i = lax.broadcasted_iota(jnp.int32, (rows, rows), axis)
        return 2 * lax.rem(i, SEQ) + i // SEQ

    def column_rows(column):
        return [pl.ds(column + 8 * r, SEQ, stride=16) for r in range(2)]

    def column_of(ts, column):
        at = column_rows(column)
        return [jnp.concatenate([wide[t, at[0], :], wide[t, at[1], :]], axis=0).astype(BF16) for t in ts]

    @pl.loop(0, 8)
    def _(column):
        apart = image_row(1) - image_row(0)
        allowed = (apart >= 0) & (apart < reach)
        out_t, weights, _ = pair_forward(*column_of(range(3), column), allowed)
        col_out_t[column] = out_t
        for h in range(2):
            col_weights[column, h] = weights[h]
        out = out_t.T
        for r, at in enumerate(column_rows(column)):
            back[at, :] = out[r * SEQ : r * SEQ + SEQ]

    res_out[...] = back[...].reshape(SEQ, 16, 128).astype(BF16)
    exchange(lambda to: remote(res_out.at[to], got_out.at[me], 7, to).start())
    got_out[me] = res_out[me]
    band_sum = sum_y(0, band_sum)

    wait_all(col_d_send, col_d_recv, 5)
    wide[3] = col_d_recv[...].astype(F32).reshape(16 * SEQ, 128)

    @pl.loop(0, 8)
    def _(column):
        values = pair_backward(
            *column_of(range(4), column), col_out_t[column], lambda h, q_t: col_weights[column, h]
        )
        for t, value in enumerate(values):
            for r, at in enumerate(column_rows(column)):
                wide[t, at, :] = value[r * SEQ : r * SEQ + SEQ]

    for t in range(3):
        res_grad[:, 16 * t : 16 * t + 16, :] = wide[t].reshape(SEQ, 16, 128).astype(BF16)

    def send_grad(to):
        remote(res_grad.at[to], got_grad.at[me], 8, to).start()

    exchange(send_grad)
    stores = [store(0, res_grad.at[me], got_grad.at[me])]
    band_sum = sum_x(0, band_sum)
    swap_w.wait()
    share_w.start()

    wait_all(res_out, got_out, 7)
    for hp in range(2):
        att[:, half + hp * 128 : half + hp * 128 + 128] = from_messages(got_out[hp * 64 : hp * 64 + 64])
    swap_column = remote(att.at[:, pl.ds(half, half)], att_other.at[:, pl.ds(half, half)], 18, me, 1 - head)
    swap_column.start()
    column_sum = sum_core(1)

    for pair in range(2):
        dk_sum[pair] = jnp.zeros((tokens + STRIDE, 128), F32)
        dv_sum[pair] = jnp.zeros((tokens + STRIDE, 128), F32)

    def band_backward(step):
        mine, span_at, allowed = band_step(step)
        for pair, lanes in enumerate(pairs):
            k = rim[0, span_at, lanes]

            def weights_of(h, q_t):
                at = 4 * pair + 2 * h
                highest, share = stats[step, at : at + 1, :], stats[step, at + 1 : at + 2, :]
                return jnp.exp(pair_scores(q_t, k, allowed, h) - highest) * share

            dq, dk, dv = pair_backward(
                q_ref[mine, lanes], k, rim[1, span_at, lanes], d_att[mine, lanes],
                att[mine, lanes].astype(F32).T, weights_of,
            )
            dq_ref[mine, lanes] = dq.astype(BF16)
            dk_sum[pair, span_at, :] += dk
            dv_sum[pair, span_at, :] += dv

    pl.loop(0, 2)(band_backward)
    for pair, lanes in enumerate(pairs):
        rim_send[0, :, lanes] = dk_sum[pair, :STRIDE, :].astype(BF16)
        rim_send[1, :, lanes] = dv_sum[pair, :STRIDE, :].astype(BF16)
    rim_back = remote(rim_send, rim_recv, 19, jnp.maximum(me - 1, 0))

    @pl.when(me > 0)
    def _():
        rim_back.start()

    @pl.when(me == SEQ - 1)
    def _():
        rim_recv[...] = jnp.zeros((2, STRIDE, half), BF16)

    column_sum = sum_y(1, column_sum)
    band_sum = sum_z(0, band_sum)
    pl.loop(2, tokens // TILE)(band_backward)
    column_sum = sum_x(1, column_sum)
    sum_end(0, band_sum)
    share_w.wait()
    swap_band.wait()
    swap_column.wait()

    @pl.loop(0, tokens // TILE)
    def _(i):
        part = pl.ds(pl.multiple_of(i * TILE, TILE), TILE)
        total = dot(att[part, :], w_ref[:, mine_c]) + dot(att_other[part, :], w_other[...])
        out_ref[part, :] = total.astype(BF16)

    stores.append(store(1, out_ref, out_to))
    stores.append(store(2, dq_ref, dq_to))
    column_sum = sum_z(1, column_sum)

    @pl.when(me > 0)
    def _():
        rim_back.wait_send()

    @pl.when(me < SEQ - 1)
    def _():
        rim_back.wait_recv()

    for t, (ref, sums) in enumerate(((dk_ref, dk_sum), (dv_ref, dv_sum))):
        for pair, lanes in enumerate(pairs):
            ref[:STRIDE, lanes] = sums[pair, STRIDE:tokens, :].astype(BF16)
            ref[STRIDE:, lanes] = (sums[pair, tokens:, :] + rim_recv[t, :, lanes].astype(F32)).astype(BF16)
    stores.append(store(3, dk_ref, dk_to))
    stores.append(store(4, dv_ref, dv_to))
    sum_end(1, column_sum)
    for copy in stores:
        copy.wait()
    wait_all(res_grad, got_grad, 8)


def result_kernel(out_ref, dq_ref, dk_ref, dv_ref, got_ref, out, dq, dk, dv, got, whole, sem):
    half = dq_ref.shape[1]
    loads, stores = [], []
    for t, band in enumerate((dq_ref, dk_ref, dv_ref)):
        part = pl.ds(16 * t, 16)
        loads.append(pltpu.make_async_copy(got_ref.at[:, part], got.at[:, part], sem.at[2 * t]))
        loads.append(pltpu.make_async_copy(band, whole.at[t, :, pl.ds(0, half)], sem.at[2 * t + 1]))
    loads.append(pltpu.make_async_copy(out_ref, whole.at[3], sem.at[6]))
    for load in loads:
        load.start()
    for t, result in enumerate((dq, dk, dv)):
        loads[2 * t].wait()
        for hp in range(2):
            lanes = slice(half + hp * 128, half + hp * 128 + 128)
            whole[t, :, lanes] = from_messages(got[hp * 64 : hp * 64 + 64, 16 * t : 16 * t + 16, :])
        loads[2 * t + 1].wait()
        stores.append(pltpu.make_async_copy(whole.at[t], result, sem.at[7 + t]))
        stores[-1].start()
    loads[6].wait()
    stores.append(pltpu.make_async_copy(whole.at[3], out, sem.at[10]))
    stores[-1].start()
    for store in stores:
        store.wait()


def local(queries, key_rows, value_rows, out_proj, grad_out, band_blocks, column_reach):
    tokens, width = queries.shape
    half = width // 2
    low = lambda *shape: pltpu.VMEM(shape, BF16)
    full = lambda *shape: pltpu.VMEM(shape, F32)
    vmem, smem = pl.BlockSpec(memory_space=pltpu.VMEM), pl.BlockSpec(memory_space=pltpu.SMEM)
    any_place = pl.BlockSpec(memory_space=pl.ANY)
    shape = jax.ShapeDtypeStruct
    result, banded = shape((tokens, width), BF16), shape((tokens, half), BF16)
    *parts, proj_grad = pl.pallas_call(
        layer_kernel,
        out_shape=(result, banded, banded, banded, shape((SEQ, 48, 128), BF16), shape((2 * width // SEQ, width), F32)),
        in_specs=[any_place] * 5 + [smem] * 2,
        out_specs=(any_place,) * 5 + (vmem,),
        scratch_shapes=[
            low(tokens, width), low(tokens, width), low(tokens, width), low(width, 2 * width), low(tokens, width),
            low(tokens, width), low(tokens, half), low(tokens, half), low(tokens, half),
            low(SEQ, 48, 128), low(SEQ, 48, 128), low(SEQ, 16, 128), low(SEQ, 16, 128), full(SEQ, 1, 128),
            low(tokens, width), low(width, width), low(2, tokens + STRIDE, half), low(2, STRIDE, half),
            low(2, STRIDE, half),
            low(tokens, width), low(2 * width, tokens), full(2, tokens + STRIDE, 128), full(2, tokens + STRIDE, 128),
            full(tokens // TILE, 8, TILE), full(4, 16 * SEQ, 128), full(16 * SEQ, 128), full(8, 2, 2 * SEQ, 2 * SEQ),
            full(8, 128, 2 * SEQ),
            low(SEQ, 16, 128), low(SEQ, 48, 128), low(SEQ, 16, 128), low(tokens, width), low(tokens, width),
            full(2, Y, Z, XH, CORES, 8, half), full(2, Y, Z, XH, 8, half), full(2, Y, Z, XH, 8, half),
            full(2, Y, Z, XH, 8, half), full(2, Z, XH, 8, half), full(2, Z, 8, half), full(2, Z, 8, half),
            full(2, Z, 8, half),
            pltpu.SemaphoreType.DMA((23,)), pltpu.SemaphoreType.DMA((23,)), pltpu.SemaphoreType.DMA((10,)),
        ],
        compiler_params=pltpu.CompilerParams(
            collective_id=0, has_side_effects=True, vmem_limit_bytes=56 * 2**20
        ),
        cost_estimate=pl.CostEstimate(flops=2 * 10**10, bytes_accessed=10 * 2**20, transcendentals=0),
    )(queries, key_rows, value_rows, out_proj, grad_out, band_blocks, column_reach)
    grads = pl.pallas_call(
        result_kernel,
        out_shape=(result,) * 4,
        in_specs=[any_place] * 5,
        out_specs=(any_place,) * 4,
        scratch_shapes=[low(SEQ, 48, 128), low(4, tokens, width), pltpu.SemaphoreType.DMA((11,))],
        compiler_params=pltpu.CompilerParams(vmem_limit_bytes=56 * 2**20),
        cost_estimate=pl.CostEstimate(flops=0, bytes_accessed=8 * 2**20, transcendentals=0),
    )(*parts)
    return (*grads, proj_grad.T)


def solution(mesh):
    tokens = P("seq", "head")
    return jax.shard_map(
        local,
        mesh=mesh,
        in_specs=(tokens, tokens, tokens, P("head", None), tokens, P("seq"), P("seq")),
        out_specs=(tokens, tokens, tokens, tokens, P("head", "seq")),
        check_vma=False,
    )
```
